32 devices in a mesh: dp: 8 (over z, x), mp: 4 (over y, core).
Axes of the slice: x: 2, y: 2, z: 4, core: 2. Of those that a mesh axis runs over, the one named last changes fastest.
Arguments:
- normed: bfloat16 [6144, 6144], P('dp', 'mp'), may hold values from -6 to 6
- pre_act: bfloat16 [6144, 24576], P('dp', 'mp'), may hold values from -6 to 6
- cotangent: bfloat16 [6144, 24576], P('dp', 'mp'), may hold values from -0.076171875 to 0.076171875
Outputs:
- up_grad: bfloat16 [6144, 24576], P('dp', 'mp')
The draws below stay inside these ranges and needn't reach their ends.
All inputs are finite; a program needn't handle non-finite values.
Results may differ from the reference program's by a relative error of at most 0.012.
Values may be sent and summed in bfloat16 or wider, within the bound.
A program may use at most 256 MiB of HBM per device.

```python
import math
import jax
import jax.numpy as jnp
from jax import lax

D = 6144
FF_WIN = 24576
TOK_DEV = 768
TOKENS = 6144


def with_spikes(drawn, stream_key, source, target, parts, factor):
    owner, partner = [(jnp.arange(drawn.shape[position]) // (drawn.shape[position] // parts)).reshape([-1 if axis == position else 1 for axis in range(drawn.ndim)]) for position in (source, target)]
    chosen = jax.random.permutation(stream_key, parts)[partner]
    strong = (owner == chosen) | (owner == (partner + parts // 2) % parts)
    return jnp.where(strong, factor * drawn, drawn)


def block_scale(own_key, shape, cuts, low, largest):
    level, own = 1.0, jax.random.fold_in(own_key, 6)
    for dim, shards_of in cuts:
        heights = jnp.exp(jax.random.uniform(jax.random.fold_in(own, dim), (shards_of,), jnp.float32, low / len(cuts), largest / len(cuts)))
        level = level * jnp.repeat(heights, shape[dim] // shards_of).reshape([-1 if axis == dim else 1 for axis in range(len(shape))])
    return level


def scatter_about(own_key, extent, deviation, reach, cuts=(), dtype=jnp.bfloat16):
    array = jax.random.normal(own_key, extent, jnp.float32) * deviation
    if len(cuts) > 0:
        array = block_scale(own_key, extent, cuts, -0.22, 0.18) * array
    return jnp.clip(array, min=-reach, max=reach).astype(dtype)


def bell_draw_with(own_key, extent, width, reach, pieces, heavy, held_as=jnp.bfloat16):
    entries = width * jax.random.normal(own_key, extent, jnp.float32)
    if pieces:
        entries = entries * block_scale(own_key, extent, pieces, -0.22, 0.18)
    return jnp.clip(with_spikes(entries, jax.random.fold_in(own_key, 3), *heavy), -reach, reach).astype(held_as)


def setup_inputs(seed: int = 0) -> dict:
    arg_keys = jax.random.split(jax.random.key(seed), 4)
    normed = bell_draw_with(arg_keys[0], (TOKENS, D), 1.0, 6.0, ((0, 8), (1, 4)), (0, 1, 8, 2.0))
    pre_act = scatter_about(arg_keys[1], (TOKENS, FF_WIN), 1.5, 6.0, ((0, 8), (1, 4)))
    cotangent = scatter_about(arg_keys[2], (TOKENS, FF_WIN), (TOKENS ** -0.5), 0.076171875, ((0, 8), (1, 4)))
    return {"normed": normed, "pre_act": pre_act, "cotangent": cotangent}


def slope_of(pre_value):
    return 0.5 * (1.0 + lax.erf(pre_value / math.sqrt(2.0))) + pre_value * jnp.exp(-0.5 * pre_value * pre_value) / math.sqrt(2.0 * math.pi)

def reference(normed, pre_act, cotangent):
    gelu_slope = slope_of(pre_act.astype(jnp.float32))
    pre_grad = (cotangent.astype(jnp.float32) * gelu_slope).astype(jnp.bfloat16)
    blocks = TOKENS // TOK_DEV
    normed_blocks = normed.reshape(blocks, TOK_DEV, D)
    grad_blocks = pre_grad.reshape(blocks, TOK_DEV, FF_WIN)

    def add_block(total, pair):
        partial_term = lax.dot_general(pair[0], pair[1], (((0,), (0,)), ((), ())), preferred_element_type=jnp.float32)
        rounded = lax.optimization_barrier(partial_term.astype(jnp.bfloat16))
        return (total + rounded.astype(jnp.float32), None)
    total, unused = lax.scan(add_block, jnp.zeros((D, FF_WIN), jnp.float32), (normed_blocks, grad_blocks))
    return total.astype(jnp.bfloat16)
```

```python
import math

import jax
import jax.numpy as jnp
from jax import lax
from jax.sharding import PartitionSpec as P

CHUNKS = 8


def slope_of(pre_value):
    return 0.5 * (1.0 + lax.erf(pre_value / math.sqrt(2.0))) + pre_value * jnp.exp(
        -0.5 * pre_value * pre_value
    ) / math.sqrt(2.0 * math.pi)


def contract_rows(left, right):
    return lax.dot_general(
        left, right, (((0,), (0,)), ((), ())), preferred_element_type=jnp.float32
    )


def build(n_dp, n_mp):
    n_hi = n_dp // 4

    def dp_pairs(hi_step, lo_flip, x_flip):
        pairs = []
        for d in range(n_dp):
            hi, lo, x = d // 4, d // 2 % 2, d % 2
            pairs.append((d, ((hi + hi_step) % n_hi * 2 + (lo ^ lo_flip)) * 2 + (x ^ x_flip)))
        return pairs

    def move(value, hi_step, lo_flip, x_flip):
        return lax.ppermute(value, "dp", dp_pairs(hi_step, lo_flip, x_flip))

    def gather_left(normed):
        lo = lax.axis_index("dp") // 2 % 2
        tokens = normed.shape[0]
        x = lax.axis_index("dp") % 2
        if n_dp == 8 and n_mp == 4:
            rows = normed.shape[1] // 2
            pieces = []
            for flip in range(2):
                pairs = []
                for d in range(n_dp):
                    hi, low, xs = d // 4, d // 2 % 2, d % 2
                    for m in range(n_mp):
                        y, core = m // 2, m % 2
                        to_d = (hi * 2 + core) * 2 + (xs ^ flip)
                        pairs.append((d * n_mp + m, to_d * n_mp + y * 2 + low))
                part = lax.dynamic_slice(normed, (0, (x ^ flip) * rows), (tokens, rows))
                pieces.append(lax.ppermute(part, ("dp", "mp"), pairs))
            full = lax.all_gather(jnp.stack(pieces), "mp", axis=0)
            return [
                [
                    [
                        lax.dynamic_index_in_dim(full, hi * 2 + (lo ^ j), 0, keepdims=False)[k]
                        for hi in range(n_hi)
                    ]
                    for k in range(2)
                ]
                for j in range(2)
            ]
        full = lax.all_gather(normed, "mp", axis=1, tiled=True)
        full = full.reshape(tokens, n_hi, 2, 2, full.shape[1] // n_dp)
        found = []
        for j in range(2):
            found.append([])
            for k in range(2):
                part = lax.dynamic_index_in_dim(full, lo ^ j, 2, keepdims=False)
                part = lax.dynamic_index_in_dim(part, x ^ k, 2, keepdims=False)
                if j or k:
                    part = move(part, 0, j, k)
                found[j].append([part[:, hi] for hi in range(n_hi)])
        return found

    def local(normed, pre_act, cotangent):
        my_hi = lax.axis_index("dp") // 4
        left = gather_left(normed)
        order = [(0, 0), (0, 1), (1, 0), (1, 1)]
        stacked = jnp.stack([jnp.concatenate([left[j][k][hi] for j, k in order]) for hi in range(n_hi)])
        width = pre_act.shape[1] // CHUNKS
        out = jnp.zeros((stacked.shape[2], pre_act.shape[1]), jnp.bfloat16)
        for i in range(CHUNKS):
            cut = slice(i * width, (i + 1) * width)
            slope = slope_of(pre_act[:, cut].astype(jnp.float32))
            own = (cotangent[:, cut].astype(jnp.float32) * slope).astype(jnp.bfloat16)
            beside = move(own, 0, 1, 0)
            across = move(own, 0, 0, 1)
            both = move(beside, 0, 0, 1)
            right = jnp.concatenate([own, across, beside, both])

            def partial(step):
                return contract_rows(
                    lax.dynamic_index_in_dim(stacked, (my_hi + step) % n_hi, 0, keepdims=False), right
                )

            sent = [move(partial(step).astype(jnp.bfloat16), step, 0, 0) for step in range(1, n_hi)]
            total = partial(0)
            for term in sent:
                total = total + term.astype(jnp.float32)
            out = lax.dynamic_update_slice(out, total.astype(jnp.bfloat16), (0, i * width))
        return out

    return local


def solution(mesh):
    return jax.shard_map(
        build(mesh.shape["dp"], mesh.shape["mp"]),
        mesh=mesh,
        in_specs=(P("dp", "mp"), P("dp", "mp"), P("dp", "mp")),
        out_specs=P("dp", "mp"),
        check_vma=False,
    )
```

```python
import math

import jax
import jax.numpy as jnp
from jax import lax
from jax.sharding import PartitionSpec as P

CHUNKS = 24
LAG = 4


def slope_of(pre_value):
    return 0.5 * (1.0 + lax.erf(pre_value / math.sqrt(2.0))) + pre_value * jnp.exp(
        -0.5 * pre_value * pre_value
    ) / math.sqrt(2.0 * math.pi)


def contract_rows(left, right):
    return lax.dot_general(
        left, right, (((0,), (0,)), ((), ())), preferred_element_type=jnp.float32
    )


def build(n_dp, n_mp):
    n_hi = n_dp // 4

    def dp_pairs(hi_step, lo_flip, x_flip):
        pairs = []
        for d in range(n_dp):
            hi, lo, x = d // 4, d // 2 % 2, d % 2
            pairs.append((d, ((hi + hi_step) % n_hi * 2 + (lo ^ lo_flip)) * 2 + (x ^ x_flip)))
        return pairs

    def move(value, hi_step, lo_flip, x_flip):
        return lax.ppermute(value, "dp", dp_pairs(hi_step, lo_flip, x_flip))

    def gather_left(normed):
        lo = lax.axis_index("dp") // 2 % 2
        tokens = normed.shape[0]
        x = lax.axis_index("dp") % 2
        if n_dp == 8 and n_mp == 4:
            rows = normed.shape[1] // 2
            pieces = [None, None]
            for flip in (1, 0):
                pairs = []
                for d in range(n_dp):
                    hi, low, xs = d // 4, d // 2 % 2, d % 2
                    for m in range(n_mp):
                        y, core = m // 2, m % 2
                        to_d = (hi * 2 + core) * 2 + (xs ^ flip)
                        pairs.append((d * n_mp + m, to_d * n_mp + y * 2 + low))
                part = lax.dynamic_slice(normed, (0, (x ^ flip) * rows), (tokens, rows))
                moved = lax.ppermute(part, ("dp", "mp"), pairs)
                pieces[flip] = lax.all_gather(moved, "mp", axis=0)
            return [
                [
                    [
                        lax.dynamic_index_in_dim(pieces[k], hi * 2 + (lo ^ j), 0, keepdims=False)
                        for hi in range(n_hi)
                    ]
                    for k in range(2)
                ]
                for j in range(2)
            ]
        full = lax.all_gather(normed, "mp", axis=1, tiled=True)
        full = full.reshape(tokens, n_hi, 2, 2, full.shape[1] // n_dp)
        found = []
        for j in range(2):
            found.append([])
            for k in range(2):
                part = lax.dynamic_index_in_dim(full, lo ^ j, 2, keepdims=False)
                part = lax.dynamic_index_in_dim(part, x ^ k, 2, keepdims=False)
                if j or k:
                    part = move(part, 0, j, k)
                found[j].append([part[:, hi] for hi in range(n_hi)])
        return found

    def local(normed, pre_act, cotangent):
        my_hi = lax.axis_index("dp") // 4
        left = gather_left(normed)
        order = [(0, 0), (0, 1), (1, 0), (1, 1)]
        stacked = jnp.stack([jnp.concatenate([left[j][k][hi] for j, k in order]) for hi in range(n_hi)])
        width = pre_act.shape[1] // CHUNKS

        def grad_chunk(i):
            cut = slice(i * width, (i + 1) * width)
            slope = slope_of(pre_act[:, cut].astype(jnp.float32))
            return (cotangent[:, cut].astype(jnp.float32) * slope).astype(jnp.bfloat16)

        def partial(step, right):
            block = lax.dynamic_index_in_dim(stacked, (my_hi + step) % n_hi, 0, keepdims=False)
            return contract_rows(block, right)

        out = jnp.zeros((stacked.shape[2], pre_act.shape[1]), jnp.bfloat16)
        own, beside, across, both, right, sent = ({} for _ in range(6))
        own[0], own[1] = grad_chunk(0), grad_chunk(1)
        across[0] = move(own[0], 0, 0, 1)
        for s in range(CHUNKS + LAG + 2):
            hop, red, done = s - 1, s - LAG, s - LAG - 2
            if s < CHUNKS:
                beside[s] = move(own[s], 0, 1, 0)
            if 0 <= hop < CHUNKS:
                both[hop] = move(beside[hop], 0, 0, 1)
            if s + 1 < CHUNKS:
                across[s + 1] = move(own[s + 1], 0, 0, 1)
            if 0 <= red < CHUNKS:
                right[red] = jnp.concatenate([own[red], across[red], beside[red], both[red]])
                sent[red] = [
                    move(partial(step, right[red]).astype(jnp.bfloat16), step, 0, 0)
                    for step in range(1, n_hi)
                ]
            if s + 2 < CHUNKS:
                own[s + 2] = grad_chunk(s + 2)
            ties = [
                (table, i)
                for table, i in (
                    (beside, s), (both, hop), (across, s), (sent, red - 1), (own, s + 1), (own, s + 2)
                )
                if i in table
            ]
            for (table, i), value in zip(ties, lax.optimization_barrier([t[i] for t, i in ties])):
                table[i] = value
            if 0 <= done < CHUNKS:
                total = partial(0, right[done])
                for term in sent[done]:
                    total = total + term.astype(jnp.float32)
                out = lax.dynamic_update_slice(out, total.astype(jnp.bfloat16), (0, done * width))
        return out

    return local


def solution(mesh):
    return jax.shard_map(
        build(mesh.shape["dp"], mesh.shape["mp"]),
        mesh=mesh,
        in_specs=(P("dp", "mp"), P("dp", "mp"), P("dp", "mp")),
        out_specs=P("dp", "mp"),
        check_vma=False,
    )
```

```python
import math

import jax
import jax.numpy as jnp
from jax import lax
from jax.sharding import PartitionSpec as P

CHUNKS = 24
LAG = 2


def slope_of(pre_value):
    return 0.5 * (1.0 + lax.erf(pre_value / math.sqrt(2.0))) + pre_value * jnp.exp(
        -0.5 * pre_value * pre_value
    ) / math.sqrt(2.0 * math.pi)


def contract_rows(left, right):
    return lax.dot_general(
        left, right, (((0,), (0,)), ((), ())), preferred_element_type=jnp.float32
    )


def build(n_dp, n_mp):
    n_hi = n_dp // 4

    def dp_pairs(hi_step, lo_flip, x_flip):
        pairs = []
        for d in range(n_dp):
            hi, lo, x = d // 4, d // 2 % 2, d % 2
            pairs.append((d, ((hi + hi_step) % n_hi * 2 + (lo ^ lo_flip)) * 2 + (x ^ x_flip)))
        return pairs

    def move(value, hi_step, lo_flip, x_flip):
        return lax.ppermute(value, "dp", dp_pairs(hi_step, lo_flip, x_flip))

    def gather_left(normed):
        lo = lax.axis_index("dp") // 2 % 2
        tokens = normed.shape[0]
        x = lax.axis_index("dp") % 2
        if n_dp == 8 and n_mp == 4:
            rows = normed.shape[1] // 2
            pieces = [None, None]
            for flip in (1, 0):
                pairs = []
                for d in range(n_dp):
                    hi, low, xs = d // 4, d // 2 % 2, d % 2
                    for m in range(n_mp):
                        y, core = m // 2, m % 2
                        to_d = (hi * 2 + core) * 2 + (xs ^ flip)
                        pairs.append((d * n_mp + m, to_d * n_mp + y * 2 + low))
                part = lax.dynamic_slice(normed, (0, (x ^ flip) * rows), (tokens, rows))
                moved = lax.ppermute(part, ("dp", "mp"), pairs)
                pieces[flip] = lax.all_gather(moved, "mp", axis=0)
            return [
                [
                    [
                        lax.dynamic_index_in_dim(pieces[k], hi * 2 + (lo ^ j), 0, keepdims=False)
                        for hi in range(n_hi)
                    ]
                    for k in range(2)
                ]
                for j in range(2)
            ]
        full = lax.all_gather(normed, "mp", axis=1, tiled=True)
        full = full.reshape(tokens, n_hi, 2, 2, full.shape[1] // n_dp)
        found = []
        for j in range(2):
            found.append([])
            for k in range(2):
                part = lax.dynamic_index_in_dim(full, lo ^ j, 2, keepdims=False)
                part = lax.dynamic_index_in_dim(part, x ^ k, 2, keepdims=False)
                if j or k:
                    part = move(part, 0, j, k)
                found[j].append([part[:, hi] for hi in range(n_hi)])
        return found

    def local(normed, pre_act, cotangent):
        my_hi = lax.axis_index("dp") // 4
        left = gather_left(normed)
        order = [(0, 0), (0, 1), (1, 0), (1, 1)]
        stacked = jnp.stack([jnp.concatenate([left[j][k][hi] for j, k in order]) for hi in range(n_hi)])
        width = pre_act.shape[1] // CHUNKS

        def grad_chunk(i):
            cut = slice(i * width, (i + 1) * width)
            slope = slope_of(pre_act[:, cut].astype(jnp.float32))
            return (cotangent[:, cut].astype(jnp.float32) * slope).astype(jnp.bfloat16)

        def partial(step, right):
            block = lax.dynamic_index_in_dim(stacked, (my_hi + step) % n_hi, 0, keepdims=False)
            return contract_rows(block, right)

        out = jnp.zeros((stacked.shape[2], pre_act.shape[1]), jnp.bfloat16)
        own, beside, across, both, right, sent = ({} for _ in range(6))
        own[0], own[1] = grad_chunk(0), grad_chunk(1)
        across[0] = move(own[0], 0, 0, 1)
        for s in range(CHUNKS + LAG + 2):
            hop, red, done = s - 1, s - LAG, s - LAG - 2
            if s < CHUNKS:
                beside[s] = move(own[s], 0, 1, 0)
            if 0 <= hop < CHUNKS:
                both[hop] = move(beside[hop], 0, 0, 1)
            if s + 1 < CHUNKS:
                across[s + 1] = move(own[s + 1], 0, 0, 1)
            if 0 <= red < CHUNKS:
                right[red] = jnp.concatenate([own[red], across[red], beside[red], both[red]])
                sent[red] = [
                    move(partial(step, right[red]).astype(jnp.bfloat16), step, 0, 0)
                    for step in range(1, n_hi)
                ]
            if s + 2 < CHUNKS:
                own[s + 2] = grad_chunk(s + 2)
            ties = [
                (table, i)
                for table, i in (
                    (beside, s), (both, hop), (across, s), (sent, red - 1), (own, s + 1), (own, s + 2)
                )
                if i in table
            ]
            for (table, i), value in zip(ties, lax.optimization_barrier([t[i] for t, i in ties])):
                table[i] = value
            if 0 <= done < CHUNKS:
                total = partial(0, right[done])
                for term in sent[done]:
                    total = total + term.astype(jnp.float32)
                out = lax.dynamic_update_slice(out, total.astype(jnp.bfloat16), (0, done * width))
        return out

    return local


def solution(mesh):
    return jax.shard_map(
        build(mesh.shape["dp"], mesh.shape["mp"]),
        mesh=mesh,
        in_specs=(P("dp", "mp"), P("dp", "mp"), P("dp", "mp")),
        out_specs=P("dp", "mp"),
        check_vma=False,
    )
```
